32 devices in a mesh: groups: 2 (over x), node: 8 (over z, y), local: 2 (over core).
Axes of the slice: x: 2, y: 2, z: 4, core: 2. Of those that a mesh axis runs over, the one named last changes fastest.
Arguments:
- tokens: bfloat16 [4096, 3584], P(('groups', 'node', 'local')), parts along dimension 0, may hold values from -6 to 6
- expert_ids: int32 [4096, 8], P(('groups', 'node', 'local')), parts along dimension 0, may hold values from 0 to 15, as said below
- gate_levels: int32 [4096, 8], P(('groups', 'node', 'local')), parts along dimension 0, may hold values from 1 to 255
- placement: int32 [16], replicated, may hold values from 0 to 15, each once
- w_gate: bfloat16 [16, 3584, 1024], P(('node', 'local')), may hold values from -0.09375 to 0.09375
- w_up: bfloat16 [16, 3584, 1024], P(('node', 'local')), may hold values from -0.09375 to 0.09375
- w_down: bfloat16 [16, 1024, 3584], P(('node', 'local')), may hold values from -0.1875 to 0.1875
Outputs:
- mixed: bfloat16 [4096, 3584], P(('groups', 'node', 'local')), parts along dimension 0
The draws below stay inside these ranges and needn't reach their ends.
There are 2 independent parts, one for each index of `groups`. The reference program is written for one: setup_inputs(seed, part) draws one part's arguments, and reference() takes and returns one part's arrays. A program takes and returns all parts, laid end to end along the dimension named above; an argument that names none is the same for every part. Nothing has to cross between parts.
Inputs may be any that keep to these rules, and one draw needn't show every extreme that they name: `expert_ids`: each row names 8 different experts. In each aligned block of 128 rows (the rows of one device) every expert is named by at least 48 and at most 80 rows, and one expert, the same in every block of a part, by exactly 80 rows. `placement`: each device of a part holds exactly one expert.
All inputs are finite; a program needn't handle non-finite values.
Results may differ from the reference program's by a relative error of at most 0.0059.
Values may be sent and summed in bfloat16 or wider, within the bound.
A program may use at most 128 MiB of HBM per device.

```python
import jax
import jax.numpy as jnp
from jax import lax

D = 3584
FFN = 1024
TOP = 8
TOK_DEV = 128
EXPERTS = 16
TOKENS = 2048
MOST = 80


def draw_expert_ids(key, part):
    key = jax.random.fold_in(key, 11)
    blocks = TOKENS // TOK_DEV
    mean_load = TOK_DEV * TOP // EXPERTS
    spread = mean_load // 4
    favored_key, block_key = jax.random.split(key)
    favored = jax.random.randint(favored_key, (), 0, EXPERTS).astype(jnp.int32)

    def one_block(block_seed):
        seeds = jax.random.split(block_seed, 4)
        ordering = jax.random.permutation(seeds[0], EXPERTS).astype(jnp.int32)
        favored_slot = jnp.sum(jnp.where(ordering == favored, lax.iota(jnp.int32, EXPERTS), 0)).astype(jnp.int32)
        pair_count = EXPERTS // 2
        deltas = jax.random.randint(seeds[1], (pair_count,), 0, spread + 1).astype(jnp.int32)
        pair_ids = lax.iota(jnp.int32, pair_count)
        favored_pair = favored_slot // 2
        deltas = jnp.where(pair_ids == favored_pair, spread, deltas)
        signs = jnp.where((pair_ids == favored_pair) & (favored_slot % 2 == 1), -1, 1).astype(jnp.int32)
        loads = mean_load + jnp.stack([signs * deltas, -signs * deltas], axis=1).reshape(EXPERTS)
        bounds = jnp.cumsum(loads).astype(jnp.int32)
        marks = lax.iota(jnp.int32, TOK_DEV * TOP)
        which = jnp.sum((marks[:, None] >= bounds[None, :]).astype(jnp.int32), axis=1)
        sequence = ordering[which]
        table = sequence.reshape(TOP, TOK_DEV).T
        row_order = jax.random.permutation(seeds[2], TOK_DEV)
        table = table[row_order]
        shifts = jax.random.randint(seeds[3], (TOK_DEV, 1), 0, TOP).astype(jnp.int32)
        columns = (lax.iota(jnp.int32, TOP)[None, :] + shifts) % TOP
        return jnp.take_along_axis(table, columns, axis=1)
    result = jax.vmap(one_block)(jax.random.split(block_key, blocks))
    return result.reshape(TOKENS, TOP).astype(jnp.int32)


def plant(drawn, stream_key, smallest, largest):
    shape = drawn.shape
    index_at = [jax.random.randint(jax.random.fold_in(stream_key, axis), (), 0, shape[axis]) for axis in range(len(shape))]
    drawn = drawn.at[tuple(index_at)].set(smallest)
    longest = shape.index(max(shape))
    index_at[longest] = (index_at[longest] + 1) % shape[longest]
    return drawn.at[tuple(index_at)].set(largest)


def steps_of(key, extent, shards, least, largest):
    def one(dim, parts):
        steps = jax.random.uniform(jax.random.fold_in(jax.random.fold_in(key, 6), dim), (parts,), jnp.float32, least / len(shards), largest / len(shards))
        return jnp.repeat(jnp.exp(steps), extent[dim] // parts).reshape((-1,) + (1,) * (len(extent) - dim - 1))

    loudness = one(*shards[0])
    for cut in shards[1:]:
        loudness = loudness * one(*cut)
    return loudness


def gaussian(own_key, dims, width, reach, pieces=(), kind=jnp.bfloat16):
    values = jax.random.normal(own_key, dims, jnp.float32) * width
    if len(pieces) > 0:
        values = steps_of(own_key, dims, pieces, -0.22, 0.18) * values
    return jnp.clip(values, min=-reach, max=reach).astype(kind)


def setup_inputs(seed: int = 0, part: int = 0) -> dict:
    arg_keys = jax.random.split(jax.random.key(seed), 8)
    own_keys = jax.random.split(jax.random.fold_in(arg_keys[7], part), 8)
    tokens = gaussian(own_keys[0], (TOKENS, D), 1.0, 6.0, ((0, 16),))
    expert_ids = draw_expert_ids(jax.random.fold_in(jax.random.fold_in(arg_keys[7], part), 71), part)
    gate_levels = plant(jax.random.randint(own_keys[2], (TOKENS, TOP), 1, 256), jax.random.fold_in(own_keys[2], 1), 1, 255).astype(jnp.int32)
    placement = jax.random.permutation(arg_keys[3], EXPERTS).astype(jnp.int32)
    w_gate = gaussian(arg_keys[4], (EXPERTS, D, FFN), D ** -0.5, 0.09375, ((0, 16),))
    w_up = gaussian(arg_keys[5], (EXPERTS, D, FFN), D ** -0.5, 0.09375, ((0, 16),))
    w_down = gaussian(arg_keys[6], (EXPERTS, FFN, D), FFN ** -0.5, 0.1875, ((0, 16),))
    return dict(tokens=tokens, expert_ids=expert_ids, gate_levels=gate_levels, placement=placement, w_gate=w_gate, w_up=w_up, w_down=w_down)


route_scale = 2.5


def reference(tokens, expert_ids, gate_levels, placement, w_gate, w_up, w_down):
    assigned = TOKENS * TOP
    flat_ids = expert_ids.reshape(assigned)
    capacity = EXPERTS * MOST

    def serve_expert(outputs, expert):
        device = jnp.sum(jnp.where(lax.iota(jnp.int32, EXPERTS) == expert, placement, 0)).astype(jnp.int32)
        chosen = jnp.nonzero(flat_ids == expert, size=capacity, fill_value=assigned)[0].astype(jnp.int32)
        token_row = jnp.minimum(chosen, assigned - 1) // TOP
        payload = tokens[token_row]
        gate_weights = lax.dynamic_index_in_dim(w_gate, device, 0, keepdims=False)
        up_weights = lax.dynamic_index_in_dim(w_up, device, 0, keepdims=False)
        down_weights = lax.dynamic_index_in_dim(w_down, device, 0, keepdims=False)
        gate_act = jnp.dot(payload, gate_weights, preferred_element_type=jnp.float32)
        up_act = jnp.dot(payload, up_weights, preferred_element_type=jnp.float32)
        hidden_act = (jax.nn.silu(gate_act) * up_act).astype(jnp.bfloat16)
        result_rows = jnp.dot(hidden_act, down_weights, preferred_element_type=jnp.float32).astype(jnp.bfloat16)
        return outputs.at[chosen].set(result_rows, mode="drop"), None

    outputs, ignored = lax.scan(serve_expert, jnp.zeros((assigned, D), jnp.bfloat16), lax.iota(jnp.int32, EXPERTS))
    picked = outputs.reshape(TOKENS, TOP, D)
    levels = gate_levels.astype(jnp.float32)
    shares = route_scale * levels / jnp.sum(levels, axis=1, keepdims=True)
    mixed_sum = jnp.zeros((TOKENS, D), jnp.float32)
    for column_index in range(TOP):
        mixed_sum = mixed_sum + shares[:, column_index, None] * picked[:, column_index].astype(jnp.float32)
    return mixed_sum.astype(jnp.bfloat16)
```

```python
import jax
import jax.numpy as jnp
from jax import lax
from jax.sharding import PartitionSpec as P

route_scale = 2.5


def device_shares(expert_ids, gate_levels, placement):
    device_count = placement.shape[0]
    levels = gate_levels.astype(jnp.float32)
    shares = route_scale * levels / jnp.sum(levels, axis=1, keepdims=True)
    expert_iota = lax.broadcasted_iota(jnp.int32, (1, 1, device_count), 2)
    target = jnp.sum(
        jnp.where(expert_ids[:, :, None] == expert_iota, placement[None, None, :], 0), axis=2
    )
    return jnp.sum(
        jnp.where(target[:, :, None] == expert_iota, shares[:, :, None], 0.0), axis=1
    )


def local(tokens, expert_ids, gate_levels, placement, w_gate, w_up, w_down):
    weight = device_shares(expert_ids, gate_levels, placement)
    me = lax.axis_index("node") * lax.axis_size("local") + lax.axis_index("local")
    rows = lax.all_gather(tokens, ("node", "local"), axis=0, tiled=True)
    weights = lax.all_gather(weight, ("node", "local"), axis=0, tiled=True)
    mine = lax.dynamic_slice_in_dim(weights, me, 1, axis=1)
    gate_act = jnp.dot(rows, w_gate[0], preferred_element_type=jnp.float32)
    up_act = jnp.dot(rows, w_up[0], preferred_element_type=jnp.float32)
    hidden_act = (jax.nn.silu(gate_act) * up_act).astype(jnp.bfloat16)
    out = jnp.dot(hidden_act, w_down[0], preferred_element_type=jnp.float32)
    part = (out * mine).astype(jnp.bfloat16)
    return lax.psum_scatter(part, ("node", "local"), scatter_dimension=0, tiled=True)


def solution(mesh):
    in_specs = (
        P(("groups", "node", "local"), None),
        P(("groups", "node", "local"), None),
        P(("groups", "node", "local"), None),
        P(),
        P(("node", "local"), None, None),
        P(("node", "local"), None, None),
        P(("node", "local"), None, None),
    )
    out_specs = P(("groups", "node", "local"), None)
    return jax.shard_map(local, mesh=mesh, in_specs=in_specs, out_specs=out_specs, check_vma=False)
```

```python
import functools

import jax
import jax.numpy as jnp
from jax import lax
from jax.experimental import pallas as pl
from jax.experimental.pallas import tpu as pltpu
from jax.sharding import PartitionSpec as P

MESH = pl.DeviceIdType.MESH
route_scale = 2.5
LANES = 128
VMEM_LIMIT = 64 * 1024 * 1024 - 256 * 1024


def device_shares(expert_ids, gate_levels, placement):
    device_count = placement.shape[0]
    levels = gate_levels.astype(jnp.float32)
    shares = route_scale * levels / jnp.sum(levels, axis=1, keepdims=True)
    expert_iota = lax.broadcasted_iota(jnp.int32, (1, 1, device_count), 2)
    target = jnp.sum(
        jnp.where(expert_ids[:, :, None] == expert_iota, placement[None, None, :], 0), axis=2
    )
    return jnp.sum(
        jnp.where(target[:, :, None] == expert_iota, shares[:, :, None], 0.0), axis=1
    )


def gathered(tokens, expert_ids, gate_levels, placement, w_gate, w_up, w_down):
    weight = device_shares(expert_ids, gate_levels, placement)
    me = lax.axis_index("node") * lax.axis_size("local") + lax.axis_index("local")
    rows = lax.all_gather(tokens, ("node", "local"), axis=0, tiled=True)
    weights = lax.all_gather(weight, ("node", "local"), axis=0, tiled=True)
    mine = lax.dynamic_slice_in_dim(weights, me, 1, axis=1)
    gate_act = jnp.dot(rows, w_gate[0], preferred_element_type=jnp.float32)
    up_act = jnp.dot(rows, w_up[0], preferred_element_type=jnp.float32)
    hidden_act = (jax.nn.silu(gate_act) * up_act).astype(jnp.bfloat16)
    out = jnp.dot(hidden_act, w_down[0], preferred_element_type=jnp.float32)
    part = (out * mine).astype(jnp.bfloat16)
    return lax.psum_scatter(part, ("node", "local"), scatter_dimension=0, tiled=True)


def kernel(
    n,
    columns,
    x_hbm,
    wg_hbm,
    wu_hbm,
    wd_hbm,
    out_ref,
    xbuf,
    wg,
    wu,
    wd,
    mine,
    sib,
    rbuf,
    stage,
    hid,
    load_sem,
    ag_send,
    ag_recv,
    xs_send,
    xs_recv,
    ys_send,
    ys_recv,
    rs_send,
    rs_recv,
):
    node = lax.axis_index("node")
    core = lax.axis_index("local")
    K = n // 2
    T = x_hbm.shape[0]
    H = T // 2
    Q = H // 2
    D = wg.shape[0]
    F = wg.shape[1]
    if columns == 2:
        side = node % 2
        level = node // 2
        pos = (1 - side) * level + side * (n - 1 - level)

        def node_at(p):
            far = p // K
            return (1 - far) * (2 * p) + far * (2 * (n - 1 - p) + 1)
    else:
        pos = node

        def node_at(p):
            return p

    right = {"node": node_at((pos + 1) % n), "local": core}
    left = {"node": node_at((pos + n - 1) % n), "local": core}
    other = {"node": node, "local": 1 - core}

    loads = [pltpu.make_async_copy(x_hbm.at[pl.ds(h * H, H)], xbuf.at[pl.ds(h * n * T, H)], load_sem.at[h]) for h in range(2)]
    loads += [
        pltpu.make_async_copy(src, dst, load_sem.at[2 + i])
        for i, (src, dst) in enumerate(((wg_hbm, wg), (wu_hbm, wu), (wd_hbm, wd)))
    ]
    for copy in loads:
        copy.start()

    barrier = pltpu.get_barrier_semaphore()
    for device in (left, right, other):
        pl.semaphore_signal(barrier, inc=1, device_id=device, device_id_type=MESH)
    pl.semaphore_wait(barrier, 3)

    def count(s):
        return 1 if s in (0, K) else 2

    def xbase(h, s):
        return h * n * T + (0 if s == 0 else T + (s - 1) * 2 * T)

    def mbase(h, s):
        return h * n * H + (0 if s == 0 else H + (s - 1) * T)

    def ag(d, h, s, sub):
        if s == 1:
            src = xbase(h, 0) + sub * Q
        else:
            src = xbase(h, s - 1) + d * H + sub * Q
        if s < K:
            dst = xbase(h, s) + d * H + sub * Q
        else:
            dst = xbase(h, s) + sub * Q
        i = ((d * 2 + h) * K + s - 1) * 2 + sub
        return pltpu.make_async_remote_copy(
            xbuf.at[pl.ds(src, Q)],
            xbuf.at[pl.ds(dst, Q)],
            ag_send.at[i],
            ag_recv.at[i],
            device_id=(right, left)[d],
            device_id_type=MESH,
        )

    def xs(h, s):
        size = count(s) * H
        i = h * (K + 1) + s
        return pltpu.make_async_remote_copy(
            xbuf.at[pl.ds(xbase(h, s), size)],
            xbuf.at[pl.ds(xbase(h, s) + size, size)],
            xs_send.at[i],
            xs_recv.at[i],
            device_id=other,
            device_id_type=MESH,
        )

    order = [(0, s) for s in range(K + 1)] + [(1, s) for s in range(K + 1)]

    def ys(h, s):
        size = count(s) * H
        i = h * (K + 1) + s
        return pltpu.make_async_remote_copy(
            stage.at[order.index((h, s)) % 2, pl.ds(0, size)],
            sib.at[pl.ds(mbase(h, s), size)],
            ys_send.at[i],
            ys_recv.at[i],
            device_id=other,
            device_id_type=MESH,
        )

    def mrow(d, h, s, sub):
        return mbase(h, s) + (d * H if s < K else 0) + sub * Q

    def rrow(d, h, s, sub):
        return h * (n - 1) * H + ((s - 1) * 2 + (d if s < K else 0)) * H + sub * Q

    def rs(d, h, s, sub):
        i = ((d * 2 + h) * K + s - 1) * 2 + sub
        return pltpu.make_async_remote_copy(
            mine.at[pl.ds(mrow(d, h, s, sub), Q)],
            rbuf.at[pl.ds(rrow(d, h, s, sub), Q)],
            rs_send.at[i],
            rs_recv.at[i],
            device_id=(left, right)[d],
            device_id_type=MESH,
        )

    def messages(s):
        return [(d, sub) for sub in range(2) for d in range(2) if s < K or sub == d]

    def arrive(h, s):
        for d, sub in ([(0, 0), (0, 1)] if s == 0 else messages(s)):
            if s > 0:
                ag(d, h, s, sub).wait_recv()
                if s < K and (d, sub) in messages(s + 1):
                    ag(d, h, s + 1, sub).start()
            else:
                for way, part in messages(1):
                    if part == sub:
                        ag(way, h, 1, sub).start()
        xs(h, s).start()

    me = node * 2 + core

    def compute(h, s):
        size = count(s) * H
        rows = 2 * size
        xs(h, s).wait_recv()
        base = xbase(h, s)
        place = order.index((h, s))
        if place >= 2:
            ys(*order[place - 2]).wait_send()
        lanes = lax.broadcasted_iota(jnp.int32, (rows, LANES), 1)
        marks = xbuf[base : base + rows, D : D + LANES].astype(jnp.float32)
        share = jnp.sum(
            jnp.where((lanes == me) | (lanes == me + LANES // 2), marks, 0.0), axis=1, keepdims=True
        )
        wide = 256

        @pl.loop(0, F // wide)
        def _(f):
            cols = pl.ds(pl.multiple_of(f * wide, wide), wide)
            x = xbuf[base : base + rows, 0:D]
            gate = jnp.dot(x, wg[:, cols], preferred_element_type=jnp.float32)
            up = jnp.dot(x, wu[:, cols], preferred_element_type=jnp.float32)
            hid[0:rows, cols] = (gate / (1.0 + jnp.exp(-gate)) * up).astype(jnp.bfloat16)

        tile = 512 if D % 512 == 0 else 256

        @pl.loop(0, D // tile)
        def _(f):
            cols = pl.ds(pl.multiple_of(f * tile, tile), tile)
            res = jnp.dot(hid[0:rows, :], wd[:, cols], preferred_element_type=jnp.float32)
            res = (res * share).astype(jnp.bfloat16)
            mine[mbase(h, s) : mbase(h, s) + size, cols] = res[0:size]
            stage[place % 2, 0:size, cols] = res[size:rows]

        ys(h, s).start()

    def reduce(h, s):
        ys(h, s).wait_recv()
        for d, sub in messages(s):
            m = mrow(d, h, s, sub)
            more = s < K and (d, sub) in messages(s + 1)
            if more:
                rs(d, h, s + 1, sub).wait_recv()
            r = rrow(d, h, s + 1, sub) if more else 0

            for a in range(0, Q, 16):
                total = mine[m + a : m + a + 16, :].astype(jnp.float32) + sib[m + a : m + a + 16, :].astype(jnp.float32)
                if more:
                    total = total + rbuf[r + a : r + a + 16, :].astype(jnp.float32)
                mine[m + a : m + a + 16, :] = total.astype(jnp.bfloat16)
            rs(d, h, s, sub).start()

    def finish(h):
        ys(h, 0).wait_recv()
        for sub in range(2):
            m = mbase(h, 0) + sub * Q
            for d in range(2):
                rs(d, h, 1, sub).wait_recv()
            r0, r1 = rrow(0, h, 1, sub), rrow(1, h, 1, sub)
            for a in range(0, Q, 16):
                total = mine[m + a : m + a + 16, :].astype(jnp.float32) + sib[m + a : m + a + 16, :].astype(jnp.float32)
                total = total + rbuf[r0 + a : r0 + a + 16, :].astype(jnp.float32)
                total = total + rbuf[r1 + a : r1 + a + 16, :].astype(jnp.float32)
                o = h * H + sub * Q + a
                out_ref[o : o + 16, :] = total.astype(jnp.bfloat16)

    loads[0].wait()
    arrive(0, 0)
    loads[1].wait()
    for copy in loads[2:]:
        copy.wait()
    for s in range(1, K + 1):
        arrive(0, s)
        if s == K - 1:
            arrive(1, 0)
        compute(0, s - 1)
    arrive(1, 1)
    compute(0, K)
    compute(1, 0)
    todo = [(0, s) for s in range(K, 0, -1)]
    for s in range(2, K + 1):
        arrive(1, s)
        if s >= K - 1:
            reduce(*todo.pop(0))
        compute(1, s - 1)
    reduce(*todo.pop(0))
    compute(1, K)
    for item in todo:
        reduce(*item)
    reduce(1, K)
    finish(0)
    for s in range(K - 1, 0, -1):
        reduce(1, s)
    finish(1)

    for h in range(2):
        for s in range(1, K + 1):
            for d, sub in messages(s):
                ag(d, h, s, sub).wait_send()
                rs(d, h, s, sub).wait_send()
        for s in range(K + 1):
            xs(h, s).wait_send()
    for item in order[-2:]:
        ys(*item).wait_send()


def ring(n, columns, tokens, expert_ids, gate_levels, placement, w_gate, w_up, w_down):
    T, D = tokens.shape
    F = w_gate.shape[2]
    K = n // 2
    weight = device_shares(expert_ids, gate_levels, placement)
    high = lax.reduce_precision(weight, 8, 7)
    low = weight - high
    room = ((0, 0), (0, LANES // 2 - placement.shape[0]))
    rows = jnp.concatenate(
        [tokens, jnp.pad(high, room).astype(jnp.bfloat16), jnp.pad(low, room).astype(jnp.bfloat16)],
        axis=1,
    )
    bf = jnp.bfloat16
    dma = pltpu.SemaphoreType.DMA
    return pl.pallas_call(
        functools.partial(kernel, n, columns),
        out_shape=jax.ShapeDtypeStruct((T, D), bf),
        in_specs=[pl.BlockSpec(memory_space=pl.ANY)] * 4,
        out_specs=pl.BlockSpec(memory_space=pltpu.VMEM),
        scratch_shapes=[
            pltpu.VMEM((2 * n * T, D + LANES), bf),
            pltpu.VMEM((D, F), bf),
            pltpu.VMEM((D, F), bf),
            pltpu.VMEM((F, D), bf),
            pltpu.VMEM((n * T, D), bf),
            pltpu.VMEM((n * T, D), bf),
            pltpu.VMEM(((n - 1) * T, D), bf),
            pltpu.VMEM((2, T, D), bf),
            pltpu.VMEM((2 * T, F), bf),
            dma((5,)),
            dma((8 * K,)),
            dma((8 * K,)),
            dma((2 * K + 2,)),
            dma((2 * K + 2,)),
            dma((2 * K + 2,)),
            dma((2 * K + 2,)),
            dma((8 * K,)),
            dma((8 * K,)),
        ],
        compiler_params=pltpu.CompilerParams(
            collective_id=0, has_side_effects=True, vmem_limit_bytes=VMEM_LIMIT
        ),
        cost_estimate=pl.CostEstimate(
            flops=12 * n * T * D * F, bytes_accessed=6 * D * F, transcendentals=2 * n * T * F
        ),
    )(rows, w_gate[0], w_up[0], w_down[0])


def solution(mesh):
    nodes = mesh.shape["node"]
    ringed = 4 <= nodes <= 8 and nodes % 2 == 0 and mesh.shape["local"] == 2
    columns = 2 if mesh.shape["groups"] == 2 else 1
    body = functools.partial(ring, nodes, columns) if ringed else gathered
    in_specs = (
        P(("groups", "node", "local"), None),
        P(("groups", "node", "local"), None),
        P(("groups", "node", "local"), None),
        P(),
        P(("node", "local"), None, None),
        P(("node", "local"), None, None),
        P(("node", "local"), None, None),
    )
    out_specs = P(("groups", "node", "local"), None)
    return jax.shard_map(body, mesh=mesh, in_specs=in_specs, out_specs=out_specs, check_vma=False)
```

```python
import functools

import jax
import jax.numpy as jnp
from jax import lax
from jax.experimental import pallas as pl
from jax.experimental.pallas import tpu as pltpu
from jax.sharding import PartitionSpec as P

MESH = pl.DeviceIdType.MESH
route_scale = 2.5
LANES = 128
VMEM_LIMIT = 64 * 1024 * 1024 - 256 * 1024


def device_shares(expert_ids, gate_levels, placement):
    device_count = placement.shape[0]
    levels = gate_levels.astype(jnp.float32)
    shares = route_scale * levels / jnp.sum(levels, axis=1, keepdims=True)
    expert_iota = lax.broadcasted_iota(jnp.int32, (1, 1, device_count), 2)
    target = jnp.sum(
        jnp.where(expert_ids[:, :, None] == expert_iota, placement[None, None, :], 0), axis=2
    )
    return jnp.sum(
        jnp.where(target[:, :, None] == expert_iota, shares[:, :, None], 0.0), axis=1
    )


def gathered(tokens, expert_ids, gate_levels, placement, w_gate, w_up, w_down):
    weight = device_shares(expert_ids, gate_levels, placement)
    me = lax.axis_index("node") * lax.axis_size("local") + lax.axis_index("local")
    rows = lax.all_gather(tokens, ("node", "local"), axis=0, tiled=True)
    weights = lax.all_gather(weight, ("node", "local"), axis=0, tiled=True)
    mine = lax.dynamic_slice_in_dim(weights, me, 1, axis=1)
    gate_act = jnp.dot(rows, w_gate[0], preferred_element_type=jnp.float32)
    up_act = jnp.dot(rows, w_up[0], preferred_element_type=jnp.float32)
    hidden_act = (jax.nn.silu(gate_act) * up_act).astype(jnp.bfloat16)
    out = jnp.dot(hidden_act, w_down[0], preferred_element_type=jnp.float32)
    part = (out * mine).astype(jnp.bfloat16)
    return lax.psum_scatter(part, ("node", "local"), scatter_dimension=0, tiled=True)


def kernel(
    n,
    columns,
    x_hbm,
    ids_ref,
    level_ref,
    where_ref,
    wg_hbm,
    wu_hbm,
    wd_hbm,
    out_ref,
    xbuf,
    mbuf,
    wg,
    wu,
    wd,
    mine,
    sib,
    rbuf,
    stage,
    hid,
    load_sem,
    ag_send,
    ag_recv,
    mk_send,
    mk_recv,
    mx_send,
    mx_recv,
    xs_send,
    xs_recv,
    ys_send,
    ys_recv,
    rs_send,
    rs_recv,
):
    node = lax.axis_index("node")
    core = lax.axis_index("local")
    me = node * 2 + core
    K = n // 2
    T = x_hbm.shape[0]
    H = T // 2
    Q = H // 2
    D = wg.shape[0]
    F = wg.shape[1]
    if columns == 2:
        side = node % 2
        level = node // 2
        pos = (1 - side) * level + side * (n - 1 - level)

        def node_at(p):
            far = p // K
            return (1 - far) * (2 * p) + far * (2 * (n - 1 - p) + 1)
    else:
        pos = node

        def node_at(p):
            return p

    right = {"node": node_at((pos + 1) % n), "local": core}
    left = {"node": node_at((pos + n - 1) % n), "local": core}
    other = {"node": node, "local": 1 - core}

    loads = []
    for h in range(2):
        part, place = pl.ds(h * H, H), pl.ds(h * n * T, H)
        loads += [pltpu.make_async_copy(x_hbm.at[part], xbuf.at[place], load_sem.at[h])]
    loads += [
        pltpu.make_async_copy(src, dst, load_sem.at[2 + i])
        for i, (src, dst) in enumerate(((wg_hbm, wg), (wu_hbm, wu), (wd_hbm, wd)))
    ]
    for copy in loads:
        copy.start()

    barrier = pltpu.get_barrier_semaphore()
    for device in (left, right, other):
        pl.semaphore_signal(barrier, inc=1, device_id=device, device_id_type=MESH)
    pl.semaphore_wait(barrier, 3)

    def count(s):
        return 1 if s in (0, K) else 2

    def xbase(h, s):
        return h * n * T + (0 if s == 0 else T + (s - 1) * 2 * T)

    def mbase(h, s):
        return h * n * H + (0 if s == 0 else H + (s - 1) * T)

    def ag(d, h, s, sub):
        if s == 1:
            src = xbase(h, 0) + sub * Q
        else:
            src = xbase(h, s - 1) + d * H + sub * Q
        if s < K:
            dst = xbase(h, s) + d * H + sub * Q
        else:
            dst = xbase(h, s) + sub * Q
        i = ((d * 2 + h) * K + s - 1) * 2 + sub
        return pltpu.make_async_remote_copy(
            xbuf.at[pl.ds(src, Q)],
            xbuf.at[pl.ds(dst, Q)],
            ag_send.at[i],
            ag_recv.at[i],
            device_id=(right, left)[d],
            device_id_type=MESH,
        )

    E = where_ref.shape[0]
    B = 2 * E

    def kbase(s):
        return 0 if s == 0 else 2 * B + (s - 1) * 4 * B

    def mk(d, s):
        src = kbase(0) if s == 1 else kbase(s - 1) + d * B
        dst = kbase(s) + (d * B if s < K else 0)
        i = d * K + s - 1
        return pltpu.make_async_remote_copy(
            mbuf.at[pl.ds(src, B)],
            mbuf.at[pl.ds(dst, B)],
            mk_send.at[i],
            mk_recv.at[i],
            device_id=(right, left)[d],
            device_id_type=MESH,
        )

    def mx(s):
        size = count(s) * B
        return pltpu.make_async_remote_copy(
            mbuf.at[pl.ds(kbase(s), size)],
            mbuf.at[pl.ds(kbase(s) + size, size)],
            mx_send.at[s],
            mx_recv.at[s],
            device_id=other,
            device_id_type=MESH,
        )

    def write_marks():
        levels = level_ref[...].astype(jnp.float32)
        shares = route_scale * levels / jnp.sum(levels, axis=1, keepdims=True)
        lanes = lax.broadcasted_iota(jnp.int32, (T, LANES), 1)
        table = jnp.zeros((T, LANES), jnp.float32)
        for j in range(ids_ref.shape[1]):
            table = table + jnp.where(ids_ref[:, j : j + 1] == lanes, shares[:, j : j + 1], 0.0)
        flipped = table.T[0:E]
        high = flipped.astype(jnp.bfloat16)
        mbuf[0:E, :] = high
        mbuf[E:B, :] = (flipped - high.astype(jnp.float32)).astype(jnp.bfloat16)

    def share_column(h, s):
        rows = lax.broadcasted_iota(jnp.int32, (B, 1), 0)
        owner = jnp.zeros((B, 1), jnp.int32)
        for e in range(E):
            owner = jnp.where((rows == e) | (rows == e + E), where_ref[e], owner)
        eye = lax.broadcasted_iota(jnp.int32, (H, T), 0) + h * H
        eye = eye == lax.broadcasted_iota(jnp.int32, (H, T), 1)
        parts = []
        for k in range(2 * count(s)):
            tile = mbuf[kbase(s) + k * B : kbase(s) + (k + 1) * B, :].astype(jnp.float32)
            row = jnp.sum(jnp.where(owner == me, tile, 0.0), axis=0, keepdims=True)
            parts.append(jnp.sum(jnp.where(eye, row, 0.0), axis=1, keepdims=True))
        return jnp.concatenate(parts, axis=0)

    def xs(h, s):
        size = count(s) * H
        i = h * (K + 1) + s
        return pltpu.make_async_remote_copy(
            xbuf.at[pl.ds(xbase(h, s), size)],
            xbuf.at[pl.ds(xbase(h, s) + size, size)],
            xs_send.at[i],
            xs_recv.at[i],
            device_id=other,
            device_id_type=MESH,
        )

    order = [(0, s) for s in range(K + 1)] + [(1, s) for s in range(K + 1)]

    def ys(h, s):
        size = count(s) * H
        i = h * (K + 1) + s
        return pltpu.make_async_remote_copy(
            stage.at[order.index((h, s)) % 2, pl.ds(0, size)],
            sib.at[pl.ds(mbase(h, s), size)],
            ys_send.at[i],
            ys_recv.at[i],
            device_id=other,
            device_id_type=MESH,
        )

    def mrow(d, h, s, sub):
        return mbase(h, s) + (d * H if s < K else 0) + sub * Q

    def rrow(d, h, s, sub):
        return h * (n - 1) * H + ((s - 1) * 2 + (d if s < K else 0)) * H + sub * Q

    def rs(d, h, s, sub):
        i = ((d * 2 + h) * K + s - 1) * 2 + sub
        return pltpu.make_async_remote_copy(
            mine.at[pl.ds(mrow(d, h, s, sub), Q)],
            rbuf.at[pl.ds(rrow(d, h, s, sub), Q)],
            rs_send.at[i],
            rs_recv.at[i],
            device_id=(left, right)[d],
            device_id_type=MESH,
        )

    def messages(s):
        return [(d, sub) for sub in range(2) for d in range(2) if s < K or sub == d]

    def arrive(h, s):
        if s > 0:
            for d, sub in messages(s):
                ag(d, h, s, sub).wait_recv()
                if s < K and (d, sub) in messages(s + 1):
                    ag(d, h, s + 1, sub).start()
        xs(h, s).start()
        if h == 0:
            for d in range(2):
                if 0 < s and (s < K or d == 0):
                    mk(d, s).wait_recv()
                if s < K - 1 or (s == K - 1 and d == 0):
                    mk(d, s + 1).start()
            mx(s).start()

    def begin(h, sub):
        for d in range(2):
            ag(d, h, 1, sub).start()


    def compute(h, s):
        size = count(s) * H
        rows = 2 * size
        xs(h, s).wait_recv()
        base = xbase(h, s)
        place = order.index((h, s))
        if place >= 2:
            ys(*order[place - 2]).wait_send()
        if h == 0:
            mx(s).wait_recv()
        share = share_column(h, s)
        wide = 256

        @pl.loop(0, F // wide)
        def _(f):
            cols = pl.ds(pl.multiple_of(f * wide, wide), wide)
            x = xbuf[base : base + rows, :]
            gate = jnp.dot(x, wg[:, cols], preferred_element_type=jnp.float32)
            up = jnp.dot(x, wu[:, cols], preferred_element_type=jnp.float32)
            hid[0:rows, cols] = (gate / (1.0 + jnp.exp(-gate)) * up).astype(jnp.bfloat16)

        tile = 512 if D % 512 == 0 else 256

        @pl.loop(0, D // tile)
        def _(f):
            cols = pl.ds(pl.multiple_of(f * tile, tile), tile)
            res = jnp.dot(hid[0:rows, :], wd[:, cols], preferred_element_type=jnp.float32)
            res = (res * share).astype(jnp.bfloat16)
            mine[mbase(h, s) : mbase(h, s) + size, cols] = res[0:size]
            stage[place % 2, 0:size, cols] = res[size:rows]

        ys(h, s).start()

    def reduce(h, s):
        ys(h, s).wait_recv()
        for d, sub in messages(s) if s == K else ((0, 1), (1, 0), (0, 0), (1, 1)):
            m = mrow(d, h, s, sub)
            more = s < K and (d, sub) in messages(s + 1)
            if more:
                rs(d, h, s + 1, sub).wait_recv()
            r = rrow(d, h, s + 1, sub) if more else 0

            for a in range(0, Q, 16):
                total = mine[m + a : m + a + 16, :].astype(jnp.float32) + sib[m + a : m + a + 16, :].astype(jnp.float32)
                if more:
                    total = total + rbuf[r + a : r + a + 16, :].astype(jnp.float32)
                mine[m + a : m + a + 16, :] = total.astype(jnp.bfloat16)
            rs(d, h, s, sub).start()

    def finish(h):
        ys(h, 0).wait_recv()
        for sub in range(2):
            m = mbase(h, 0) + sub * Q
            for d in range(2):
                rs(d, h, 1, sub).wait_recv()
            r0, r1 = rrow(0, h, 1, sub), rrow(1, h, 1, sub)
            for a in range(0, Q, 16):
                total = mine[m + a : m + a + 16, :].astype(jnp.float32) + sib[m + a : m + a + 16, :].astype(jnp.float32)
                total = total + rbuf[r0 + a : r0 + a + 16, :].astype(jnp.float32)
                total = total + rbuf[r1 + a : r1 + a + 16, :].astype(jnp.float32)
                o = h * H + sub * Q + a
                out_ref[o : o + 16, :] = total.astype(jnp.bfloat16)

    loads[0].wait()
    begin(0, 0)
    write_marks()
    arrive(0, 0)
    for copy in loads[1:]:
        copy.wait()
    for d in range(2):
        ag(d, 0, 1, 0).wait_send()
    begin(0, 1)
    for s in range(1, K + 1):
        arrive(0, s)
        if s == K - 1:
            begin(1, 0)
            arrive(1, 0)
        if s == K:
            begin(1, 1)
        compute(0, s - 1)
    arrive(1, 1)
    compute(0, K)
    compute(1, 0)
    todo = [(0, s) for s in range(K, 0, -1)]
    for s in range(2, K + 1):
        arrive(1, s)
        if s >= K - 1:
            reduce(*todo.pop(0))
        compute(1, s - 1)
    reduce(*todo.pop(0))
    compute(1, K)
    for item in todo:
        reduce(*item)
    reduce(1, K)
    finish(0)
    for s in range(K - 1, 0, -1):
        reduce(1, s)
    finish(1)

    for h in range(2):
        for s in range(1, K + 1):
            for d, sub in messages(s):
                if (h, s, sub) != (0, 1, 0):
                    ag(d, h, s, sub).wait_send()
                rs(d, h, s, sub).wait_send()
        for s in range(K + 1):
            xs(h, s).wait_send()
    for s in range(1, K + 1):
        for d in range(2):
            if s < K or d == 0:
                mk(d, s).wait_send()
    for s in range(K + 1):
        mx(s).wait_send()
    for item in order[-2:]:
        ys(*item).wait_send()


def ring(n, columns, tokens, expert_ids, gate_levels, placement, w_gate, w_up, w_down):
    T, D = tokens.shape
    F = w_gate.shape[2]
    K = n // 2
    E = placement.shape[0]
    bf = jnp.bfloat16
    dma = pltpu.SemaphoreType.DMA
    return pl.pallas_call(
        functools.partial(kernel, n, columns),
        out_shape=jax.ShapeDtypeStruct((T, D), bf),
        in_specs=[pl.BlockSpec(memory_space=pl.ANY)]
        + [pl.BlockSpec(memory_space=pltpu.VMEM)] * 2
        + [pl.BlockSpec(memory_space=pltpu.SMEM)]
        + [pl.BlockSpec(memory_space=pl.ANY)] * 3,
        out_specs=pl.BlockSpec(memory_space=pltpu.VMEM),
        scratch_shapes=[
            pltpu.VMEM((2 * n * T, D), bf),
            pltpu.VMEM((4 * n * E, T), bf),
            pltpu.VMEM((D, F), bf),
            pltpu.VMEM((D, F), bf),
            pltpu.VMEM((F, D), bf),
            pltpu.VMEM((n * T, D), bf),
            pltpu.VMEM((n * T, D), bf),
            pltpu.VMEM(((n - 1) * T, D), bf),
            pltpu.VMEM((2, T, D), bf),
            pltpu.VMEM((2 * T, F), bf),
            dma((5,)),
            dma((8 * K,)),
            dma((8 * K,)),
            dma((2 * K,)),
            dma((2 * K,)),
            dma((K + 1,)),
            dma((K + 1,)),
            dma((2 * K + 2,)),
            dma((2 * K + 2,)),
            dma((2 * K + 2,)),
            dma((2 * K + 2,)),
            dma((8 * K,)),
            dma((8 * K,)),
        ],
        compiler_params=pltpu.CompilerParams(
            collective_id=0, has_side_effects=True, vmem_limit_bytes=VMEM_LIMIT
        ),
        cost_estimate=pl.CostEstimate(
            flops=12 * n * T * D * F, bytes_accessed=6 * D * F, transcendentals=2 * n * T * F
        ),
    )(tokens, expert_ids, gate_levels, placement, w_gate[0], w_up[0], w_down[0])


def solution(mesh):
    nodes = mesh.shape["node"]
    ringed = 4 <= nodes <= 8 and nodes % 2 == 0 and mesh.shape["local"] == 2
    columns = 2 if mesh.shape["groups"] == 2 else 1
    body = functools.partial(ring, nodes, columns) if ringed else gathered
    in_specs = (
        P(("groups", "node", "local"), None),
        P(("groups", "node", "local"), None),
        P(("groups", "node", "local"), None),
        P(),
        P(("node", "local"), None, None),
        P(("node", "local"), None, None),
        P(("node", "local"), None, None),
    )
    out_specs = P(("groups", "node", "local"), None)
    return jax.shard_map(body, mesh=mesh, in_specs=in_specs, out_specs=out_specs, check_vma=False)
```
